512 devices in a mesh: ctx: 128 (over z, x, y_hi), head: 4 (over y_lo, core).
Axes of the slice: x: 4, y: 4 (y_hi: 2, y_lo: 2; y = y_hi * 2 + y_lo), z: 16, core: 2. Of those that a mesh axis runs over, the one named last changes fastest.
Arguments:
- win_q: bfloat16 [16384, 4096], P('ctx', 'head'), may hold values from -5.5 to 5.5, as said below
- win_k: bfloat16 [16384, 512], P(('ctx', 'head')), may hold values from -5.5 to 5.5, as said below
- win_v: bfloat16 [16384, 512], P(('ctx', 'head')), may hold values from -6 to 6
- win_dout: bfloat16 [16384, 4096], P('ctx', 'head'), may hold values from -32 to 32
- full_q: bfloat16 [16384, 4096], P('ctx', 'head'), may hold values from -5.5 to 5.5, as said below
- full_k: bfloat16 [16384, 512], P(('ctx', 'head')), may hold values from -5.5 to 5.5, as said below
- full_v: bfloat16 [16384, 512], P(('ctx', 'head')), may hold values from -6 to 6
- full_dout: bfloat16 [16384, 4096], P('ctx', 'head'), may hold values from -32 to 32
- sinks: float32 [2, 64], P(None, 'head'), may hold values from 0 to 3
- segments: int32 [16384], replicated, may hold values from 0 to 31, never falling along the last dimension, each value on 1 to 768 neighbouring positions
Outputs:
- win_dq: bfloat16 [16384, 4096], P('ctx', 'head')
- win_dk: bfloat16 [16384, 512], P(('ctx', 'head'))
- win_dv: bfloat16 [16384, 512], P(('ctx', 'head'))
- full_dq: bfloat16 [16384, 4096], P('ctx', 'head')
- full_dk: bfloat16 [16384, 512], P(('ctx', 'head'))
- full_dv: bfloat16 [16384, 512], P(('ctx', 'head'))
- sink_grads: float32 [2, 64], P(None, 'head')
The draws below stay inside these ranges and needn't reach their ends.
Inputs may be any that keep to these rules, and one draw needn't show every extreme that they name: `segments`: document numbers never fall along the sequence, every number is used, each document has 1 to 768 tokens and one has exactly 768. `win_q`: query features. `win_k`: key features. `full_q`: query features. `full_k`: key features.
All inputs are finite; a program needn't handle non-finite values.
Results may differ from the reference program's by a relative error of at most 0.012.
The reference program's roundings to bfloat16 on the way (of `weights` and `score_grads`) count: a program that leaves them out, or rounds other values in their place, can miss the bound.
Values may be sent and summed in bfloat16 or wider, within the bound.
No kernel may reach another device: no remote copies, remote signals or barrier semaphores. Data moves between devices by JAX's collectives and lax.ppermute only.
A program may use at most 64 MiB of HBM per device.

```python
import math
import jax
import jax.numpy as jnp
import numpy as np
from jax import lax

HEADS = 64
KV_HEADS = 8
HEAD_DIM = 64
WINDOW = 128
CYCLE = 4
TOK_DEV = 128
GROUP = 8
TOKENS = 16384
DOCS = 32
DOC_MOST = 768


def drawn_pair(seed_key):
    query_key, key_key = jax.random.split(seed_key, 2)
    query_base = jnp.clip(jax.random.normal(query_key, (TOKENS, KV_HEADS, GROUP, HEAD_DIM), jnp.float32), -5.5, 5.5)
    key_base = jnp.clip(jax.random.normal(key_key, (TOKENS, KV_HEADS, HEAD_DIM), jnp.float32), -5.5, 5.5)
    return (query_base.reshape(TOKENS, HEADS * HEAD_DIM), key_base.reshape(TOKENS, KV_HEADS * HEAD_DIM))


def draw_win_q(key, part):
    return drawn_pair(jax.random.fold_in(key, 11))[0].astype(jnp.bfloat16)


def draw_win_k(key, part):
    return drawn_pair(jax.random.fold_in(key, 11))[1].astype(jnp.bfloat16)


def draw_full_q(key, part):
    return drawn_pair(jax.random.fold_in(key, 23))[0].astype(jnp.bfloat16)


def draw_full_k(key, part):
    return drawn_pair(jax.random.fold_in(key, 23))[1].astype(jnp.bfloat16)


def levels(own_key, extent, pieces, smallest, largest):
    factor_of, own = 1.0, jax.random.fold_in(own_key, 6)
    for dim, blocks in pieces:
        heights = jnp.exp(jax.random.uniform(jax.random.fold_in(own, dim), (blocks,), jnp.float32, smallest / len(pieces), largest / len(pieces)))
        factor_of = factor_of * jnp.repeat(heights, extent[dim] // blocks).reshape([-1 if axis == dim else 1 for axis in range(len(extent))])
    return factor_of


def profile(count, total, bound, lean):
    loads = [(1 << 20) // math.isqrt(grade ** lean) + 1 for grade in range(2, count + 1)]
    spare, counts = total - bound - (count - 1), [1] * (count - 1)
    while spare > 0:
        movable = [i for i in range(count - 1) if counts[i] < bound]
        pool, remaining = sum([loads[i] for i in movable]), spare
        for i in movable:
            extra = min(bound - counts[i], max(1, remaining * loads[i] // pool), spare)
            counts[i] = counts[i] + extra
            spare = spare - extra
    return np.array([bound] + counts)


def uneven_parts(stream_key, number_of, total, limit, skew):
    if number_of == 2:
        one = jax.random.randint(stream_key, (), max(1, total - limit), min(limit, total - 1) + 1)
        return jnp.stack([one, total - one])
    sizes = jnp.asarray(profile(number_of, total, limit, skew), jnp.int32)
    pairs = (number_of - 1) // 2
    donor, receiver = sizes[1:1 + 2 * pairs:2], sizes[2:2 + 2 * pairs:2]
    slack = jnp.minimum(donor - 1, limit - receiver)
    passed = jax.random.randint(jax.random.fold_in(stream_key, 1), (pairs,), 0, 1 << 20) % (slack + 1)
    sizes = sizes.at[1:1 + 2 * pairs:2].set(donor - passed).at[2:2 + 2 * pairs:2].set(receiver + passed)
    return sizes[jax.random.permutation(jax.random.fold_in(stream_key, 2), number_of)]


def gaussian(own_key, shape, scale, most, cuts=(), kind=jnp.bfloat16):
    values = scale * jax.random.normal(own_key, shape, jnp.float32)
    if cuts:
        values = values * levels(own_key, shape, cuts, -0.22, 0.18)
    return jnp.clip(values, -most, most).astype(kind)


def setup_inputs(seed: int = 0) -> dict:
    arg_keys = jax.random.split(jax.random.key(seed), 11)
    win_q = draw_win_q(jax.random.fold_in(arg_keys[10], 71), 0)
    win_k = draw_win_k(jax.random.fold_in(arg_keys[10], 71), 0)
    win_v = gaussian(arg_keys[2], (TOKENS, KV_HEADS * HEAD_DIM), 1.0, 6.0, ((0, 512),))
    win_dout = gaussian(arg_keys[3], (TOKENS, HEADS * HEAD_DIM), 6.0, 32.0, ((0, 128), (1, 4)))
    full_q = draw_full_q(jax.random.fold_in(arg_keys[10], 71), 0)
    full_k = draw_full_k(jax.random.fold_in(arg_keys[10], 71), 0)
    full_v = gaussian(arg_keys[6], (TOKENS, KV_HEADS * HEAD_DIM), 1.0, 6.0, ((0, 512),))
    full_dout = gaussian(arg_keys[7], (TOKENS, HEADS * HEAD_DIM), 6.0, 32.0, ((0, 128), (1, 4)))
    sinks = jnp.clip(3.0 * jax.random.uniform(arg_keys[8], (2, HEADS), jnp.float32) ** levels(arg_keys[8], (2, HEADS), ((1, 4),), -0.2, 0.2), 0.0, 3.0)
    segments = jnp.searchsorted(jnp.cumsum(uneven_parts(arg_keys[9], DOCS, TOKENS, DOC_MOST, 1)), jnp.arange(TOKENS), side="right").astype(jnp.int32)
    return dict(win_q=win_q, win_k=win_k, win_v=win_v, win_dout=win_dout, full_q=full_q, full_k=full_k, full_v=full_v, full_dout=full_dout, sinks=sinks, segments=segments)


NEG = -1.0e30


def attention_grads(queries, cotangent, key_rows, value_rows, allowed, sink_logit, scaling):
    query_f = queries.astype(jnp.float32)
    cotan_f = cotangent.astype(jnp.float32)
    key_f = key_rows.astype(jnp.float32)
    value_f = value_rows.astype(jnp.float32)
    raw = jnp.einsum("qhgd,khd->hgqk", query_f, key_f)
    scores = jnp.where(allowed[None, None], scaling * raw, NEG)
    row_max = jnp.maximum(jnp.max(scores, axis=-1), sink_logit[..., None])
    exponent = jnp.exp(scores - row_max[..., None])
    sink_term = jnp.exp(sink_logit[..., None] - row_max)
    row_total = jnp.sum(exponent, axis=-1) + sink_term
    softmax = exponent / row_total[..., None]
    weights = lax.optimization_barrier(softmax.astype(jnp.bfloat16)).astype(jnp.float32)
    output = jnp.einsum("hgqk,khd->qhgd", weights, value_f)
    row_delta = jnp.transpose(jnp.sum(cotan_f * output, axis=-1), (1, 2, 0))
    weight_grads = jnp.einsum("qhgd,khd->hgqk", cotan_f, value_f)
    score_grads = softmax * (weight_grads - row_delta[..., None])
    score_grads = lax.optimization_barrier(score_grads.astype(jnp.bfloat16)).astype(jnp.float32)
    query_grads = scaling * jnp.einsum("hgqk,khd->qhgd", score_grads, key_f)
    key_grads = scaling * jnp.einsum("hgqk,qhgd->khd", score_grads, query_f)
    value_grads = jnp.einsum("hgqk,qhgd->khd", weights, cotan_f)
    sink_grads = -jnp.sum(sink_term / row_total * row_delta, axis=-1)
    return query_grads, key_grads, value_grads, sink_grads


def layer_pass(queries, key_all, value_all, cotangent, sink_logit, segments, scaling, reach, banded):
    blocks = TOKENS // TOK_DEV
    width = TOK_DEV + reach
    kv_width = KV_HEADS * HEAD_DIM
    key_pad = jnp.concatenate([jnp.zeros((reach, kv_width), key_all.dtype), key_all])
    value_pad = jnp.concatenate([jnp.zeros((reach, kv_width), value_all.dtype), value_all])
    seg_pad = jnp.concatenate([jnp.full((reach,), -1, jnp.int32), segments])

    def one_block(index):
        row_start = (index * TOK_DEV).astype(jnp.int32)
        query_rows = lax.dynamic_slice_in_dim(queries, row_start, TOK_DEV).reshape(TOK_DEV, KV_HEADS, GROUP, HEAD_DIM)
        cotan_rows = lax.dynamic_slice_in_dim(cotangent, row_start, TOK_DEV).reshape(TOK_DEV, KV_HEADS, GROUP, HEAD_DIM)
        key_rows = lax.dynamic_slice_in_dim(key_pad, row_start, width).reshape(width, KV_HEADS, HEAD_DIM)
        value_rows = lax.dynamic_slice_in_dim(value_pad, row_start, width).reshape(width, KV_HEADS, HEAD_DIM)
        query_pos = row_start + jnp.arange(TOK_DEV, dtype=jnp.int32)
        key_pos = row_start - reach + jnp.arange(width, dtype=jnp.int32)
        query_seg = lax.dynamic_slice_in_dim(segments, row_start, TOK_DEV)
        key_seg = lax.dynamic_slice_in_dim(seg_pad, row_start, width)
        allowed = (key_pos[None, :] <= query_pos[:, None]) & (key_seg[None, :] == query_seg[:, None])
        if not banded:
            allowed = allowed & (key_pos[None, :] > query_pos[:, None] - WINDOW)
        return attention_grads(query_rows, cotan_rows, key_rows, value_rows, allowed, sink_logit, scaling)

    query_grads, key_grads, value_grads, sink_grads = lax.map(one_block, jnp.arange(blocks, dtype=jnp.int32))
    query_out = query_grads.reshape(TOKENS, HEADS * HEAD_DIM).astype(jnp.bfloat16)
    sink_out = jnp.sum(sink_grads, axis=0).reshape(HEADS)
    results = []
    for grads in (key_grads, value_grads):
        grads = grads.reshape(blocks, width, kv_width)
        if banded:
            parts = grads.reshape(blocks, CYCLE + 1, TOK_DEV, kv_width)
            total = jnp.zeros((blocks, TOK_DEV, kv_width), jnp.float32)
            for offset in range(CYCLE + 1):
                lag = CYCLE - offset
                piece = parts[lag:, offset]
                total = total + jnp.concatenate([piece, jnp.zeros((lag, TOK_DEV, kv_width), jnp.float32)])
        else:
            edge_part = grads[:, :WINDOW]
            own_part = grads[:, WINDOW:]
            moved = jnp.concatenate([edge_part[1:], jnp.zeros((1, WINDOW, kv_width), jnp.float32)])
            total = own_part + jnp.pad(moved, ((0, 0), (TOK_DEV - WINDOW, 0), (0, 0)))
        results.append(total.reshape(TOKENS, kv_width).astype(jnp.bfloat16))
    return query_out, results[0], results[1], sink_out


def reference(win_q, win_k, win_v, win_dout, full_q, full_k, full_v, full_dout, sinks, segments):
    scaling = HEAD_DIM ** -0.5
    win_dq, win_dk, win_dv, win_sink = layer_pass(win_q, win_k, win_v, win_dout, sinks[0].reshape(KV_HEADS, GROUP), segments, scaling, WINDOW, False)
    full_dq, full_dk, full_dv, full_sink = layer_pass(full_q, full_k, full_v, full_dout, sinks[1].reshape(KV_HEADS, GROUP), segments, scaling, CYCLE * TOK_DEV, True)
    return (win_dq, win_dk, win_dv, full_dq, full_dk, full_dv, jnp.stack([win_sink, full_sink]))
```

```python
import jax
import jax.numpy as jnp
from jax import lax
from jax.experimental import pallas as pl
from jax.experimental.pallas import tpu as pltpu
from jax.sharding import PartitionSpec as P

HEAD_DIM = 64
CYCLE = 4
BLOCK = 128
PAIRS = 4
NEG = -1e30
VMEM = pl.BlockSpec(memory_space=pltpu.VMEM)
SMEM = pl.BlockSpec(memory_space=pltpu.SMEM)
BF16, F32 = jnp.bfloat16, jnp.float32


def passed_along(shard, axis, by):
    size = lax.axis_size(axis)
    pairs = [(i, i + by) for i in range(size) if 0 <= i + by < size]
    return lax.ppermute(shard, axis, pairs)


def low_lanes(rows):
    return lax.broadcasted_iota(jnp.int32, (rows, 128), 1) < 64


def both_ways(tile):
    turned = pltpu.roll(tile, 64, 1)
    low = low_lanes(tile.shape[0])
    return jnp.where(low, tile, turned), jnp.where(low, turned, tile)


def pair_rows(tile):
    low = low_lanes(128)
    zero = jnp.zeros_like(tile)
    return jnp.concatenate([jnp.where(low, tile, zero), jnp.where(low, zero, tile)], axis=0)


def dot(a, b, contract):
    return lax.dot_general(a, b, (contract, ((), ())), preferred_element_type=F32)


def build_bias(bias, seg_ref, me, blocks, windowed):
    seg_q = jnp.broadcast_to(seg_ref[pl.ds(me, 1), :], (128, 128))
    key_row = lax.broadcasted_iota(jnp.int32, (128, 128), 0)
    query_col = lax.broadcasted_iota(jnp.int32, (128, 128), 1)
    for b in range(blocks):
        lag = blocks - 1 - b
        at = me - lag
        seg_row = jnp.broadcast_to(seg_ref[pl.ds(jnp.maximum(at, 0), 1), :], (128, 128))
        seg_k = jnp.transpose(seg_row.astype(F32)).astype(jnp.int32)
        allowed = (seg_k == seg_q) & (at >= 0)
        if lag == 0:
            allowed = allowed & (key_row <= query_col)
        elif windowed:
            allowed = allowed & (key_row > query_col)
        tile = jnp.where(allowed, 0.0, NEG).astype(F32)
        bias[b * 128 : (b + 1) * 128, :] = jnp.concatenate([tile, tile], axis=1)


def layer(layer_id, sinks_ref, q_ref, do_ref, keys, values, bias, kd, vd, kt, ws, dss, dq_ref, sink_acc):
    blocks = len(keys)
    rows = blocks * 128
    for b in range(blocks):
        span = slice(b * 128, (b + 1) * 128)
        key = keys[b]().astype(F32) * (HEAD_DIM**-0.5)
        k0, k1 = both_ways(key)
        kd[0, span, :] = k0.astype(BF16)
        kd[1, span, :] = k1.astype(BF16)
        turned = jnp.transpose(key).astype(BF16)
        kt[0, :, span] = turned[:64]
        kt[1, :, span] = turned[64:]
        v0, v1 = both_ways(values[b]().astype(F32))
        vd[0, span, :] = v0.astype(BF16)
        vd[1, span, :] = v1.astype(BF16)
    lane = lax.broadcasted_iota(jnp.int32, (1, 256), 1)
    sums = []
    for g in range(2):
        q2s, do2s = [], []
        for j in range(PAIRS):
            p = g * PAIRS + j
            q2 = pair_rows(q_ref[:, p * 128 : (p + 1) * 128])
            do2 = pair_rows(do_ref[:, p * 128 : (p + 1) * 128])
            q2s.append(q2)
            do2s.append(do2)
            sink = jnp.where(lane < 128, sinks_ref[layer_id, 2 * p], sinks_ref[layer_id, 2 * p + 1])
            s = dot(kd[g, :rows, :], q2, ((1,), (1,))) + bias[:rows, :]
            m = jnp.maximum(jnp.max(s, axis=0, keepdims=True), sink)
            e = jnp.exp(s - m)
            sink_term = jnp.exp(sink - m)
            inverse = 1.0 / (jnp.sum(e, axis=0, keepdims=True) + sink_term)
            pr = e * inverse
            dp = dot(vd[g, :rows, :], do2, ((1,), (1,)))
            delta = jnp.sum(pr * dp, axis=0, keepdims=True)
            ws[:rows, j * 256 : (j + 1) * 256] = pr.astype(BF16)
            dss[:rows, j * 256 : (j + 1) * 256] = (pr * (dp - delta)).astype(BF16)
            grad = -(sink_term * inverse) * delta
            at = layer_id * 16 + 2 * p
            sink_acc[at : at + 1, :] = grad[:, :128]
            sink_acc[at + 1 : at + 2, :] = grad[:, 128:]
        q_all = jnp.concatenate(q2s, axis=0)
        do_all = jnp.concatenate(do2s, axis=0)
        dk = dot(dss[:rows, :], q_all, ((1,), (0,)))
        dv = dot(ws[:rows, :], do_all, ((1,), (0,)))
        sums.append((dk + pltpu.roll(dk, 64, 1), dv + pltpu.roll(dv, 64, 1)))
        dqt = dot(kt[g, :, :rows], dss[:rows, :], ((1,), (0,)))
        for j in range(PAIRS):
            p = g * PAIRS + j
            both = jnp.concatenate([dqt[:, j * 256 : j * 256 + 128], dqt[:, j * 256 + 128 : j * 256 + 256]], axis=0)
            dq_ref[:, p * 128 : (p + 1) * 128] = jnp.transpose(both).astype(BF16)
    low = low_lanes(rows)
    dk = jnp.where(low, sums[0][0], sums[1][0]) * (HEAD_DIM**-0.5)
    dv = jnp.where(low, sums[0][1], sums[1][1])
    return dk, dv


def attention_kernel(
    me_ref, sinks_ref, seg_ref, wq_ref, wdo_ref, fq_ref, fdo_ref, own, far1, far2, far3, far4,
    wdq_ref, fdq_ref, mine, back1, back2, back3, back4, sink_ref,
    bias, kd, vd, kt, ws, dss, sink_acc,
):
    me = me_ref[0]
    sink_acc[...] = jnp.zeros_like(sink_acc)

    def tile(ref, at):
        return lambda: ref[:, at : at + 128]

    build_bias(bias, seg_ref, me, 2, True)
    dk, dv = layer(
        0, sinks_ref, wq_ref, wdo_ref, [tile(far1, 0), tile(own, 0)], [tile(far1, 128), tile(own, 128)],
        bias, kd, vd, kt, ws, dss, wdq_ref, sink_acc,
    )
    back1[:, 0:128] = dk[:128].astype(BF16)
    back1[:, 128:256] = dv[:128].astype(BF16)
    mine[:, 0:128] = dk[128:]
    mine[:, 128:256] = dv[128:]
    build_bias(bias, seg_ref, me, CYCLE + 1, False)
    dk, dv = layer(
        1, sinks_ref, fq_ref, fdo_ref,
        [tile(far4, 0), tile(far3, 0), tile(far2, 0), tile(far1, 256), tile(own, 256)],
        [tile(far4, 128), tile(far3, 128), tile(far2, 128), tile(far1, 384), tile(own, 384)],
        bias, kd, vd, kt, ws, dss, fdq_ref, sink_acc,
    )
    for b, ref in enumerate((back4, back3, back2)):
        ref[:, 0:128] = dk[b * 128 : (b + 1) * 128].astype(BF16)
        ref[:, 128:256] = dv[b * 128 : (b + 1) * 128].astype(BF16)
    back1[:, 256:384] = dk[384:512].astype(BF16)
    back1[:, 384:512] = dv[384:512].astype(BF16)
    mine[:, 256:384] = dk[512:]
    mine[:, 384:512] = dv[512:]
    total = jnp.sum(jnp.transpose(sink_acc[...]), axis=0, keepdims=True)
    sink_ref[...] = jnp.broadcast_to(total, sink_ref.shape)


def attention(me, sinks, seg, wq, wdo, fq, fdo, own, far1, far2, far3, far4):
    rows = (CYCLE + 1) * 128
    shape = jax.ShapeDtypeStruct
    return pl.pallas_call(
        attention_kernel,
        out_shape=(
            shape((128, 1024), BF16), shape((128, 1024), BF16), shape((128, 512), F32), shape((128, 512), BF16),
            shape((128, 256), BF16), shape((128, 256), BF16), shape((128, 256), BF16), shape((128, 128), F32),
        ),
        in_specs=[SMEM, SMEM] + [VMEM] * 10,
        out_specs=[VMEM] * 8,
        scratch_shapes=[
            pltpu.VMEM((rows, 256), F32),
            pltpu.VMEM((2, rows, 128), BF16),
            pltpu.VMEM((2, rows, 128), BF16),
            pltpu.VMEM((2, 64, rows), BF16),
            pltpu.VMEM((rows, 1024), BF16),
            pltpu.VMEM((rows, 1024), BF16),
            pltpu.VMEM((128, 128), F32),
        ],
        compiler_params=pltpu.CompilerParams(vmem_limit_bytes=40 << 20),
        cost_estimate=pl.CostEstimate(flops=3_000_000_000, bytes_accessed=4_000_000, transcendentals=2_000_000),
    )(me, sinks, seg, wq, wdo, fq, fdo, own, far1, far2, far3, far4)


def pack_kernel(wk, wv, fk, fv, out):
    for a, ref in enumerate((wk, wv, fk, fv)):
        for t in range(4):
            out[t * 32 : (t + 1) * 32, a * 128 : (a + 1) * 128] = ref[:, t * 128 : (t + 1) * 128]


def sum_kernel(mine, back1, back2, back3, back4, out):
    out[:, :256] = (mine[:, :256] + back1[:, :256].astype(F32)).astype(BF16)
    banded = back2[...].astype(F32) + back3[...].astype(F32) + back4[...].astype(F32)
    out[:, 256:] = (mine[:, 256:] + back1[:, 256:].astype(F32) + banded).astype(BF16)


def unpack_kernel(grads, sink_terms, wk, wv, fk, fv, sinks):
    for a, ref in enumerate((wk, wv, fk, fv)):
        for t in range(4):
            ref[:, t * 128 : (t + 1) * 128] = grads[t * 32 : (t + 1) * 32, a * 128 : (a + 1) * 128]
    total = jnp.sum(sink_terms[...], axis=0, keepdims=True)
    sinks[0:1, :] = total[:, 0:16]
    sinks[1:2, :] = total[:, 16:32]


def local_call(kernel, out_shape, args):
    return pl.pallas_call(
        kernel,
        out_shape=out_shape,
        in_specs=[VMEM] * len(args),
        out_specs=jax.tree.map(lambda _: VMEM, out_shape),
        compiler_params=pltpu.CompilerParams(vmem_limit_bytes=4 << 20),
        cost_estimate=pl.CostEstimate(flops=100_000, bytes_accessed=500_000, transcendentals=0),
    )(*args)


def body(win_q, win_k, win_v, win_dout, full_q, full_k, full_v, full_dout, sinks, segments):
    shape = jax.ShapeDtypeStruct
    packed = local_call(pack_kernel, shape((128, 512), BF16), (win_k, win_v, full_k, full_v))
    own = lax.all_to_all(packed, "head", split_axis=0, concat_axis=0, tiled=True)
    banded = own[:, 256:]
    far1 = passed_along(own, "ctx", 1)
    far2, far3, far4 = (passed_along(banded, "ctx", by) for by in (2, 3, 4))
    me = lax.axis_index("ctx").astype(jnp.int32).reshape(1)
    win_dq, full_dq, mine, back1, back2, back3, back4, sink_rows = attention(
        me, sinks, segments.reshape(128, 128), win_q, win_dout, full_q, full_dout, own, far1, far2, far3, far4
    )
    sink_terms = lax.all_to_all(sink_rows, "ctx", split_axis=0, concat_axis=0, tiled=True)
    backs = [passed_along(back, "ctx", -by) for by, back in enumerate((back1, back2, back3, back4), 1)]
    summed = local_call(sum_kernel, shape((128, 512), BF16), (mine, *backs))
    grads = lax.all_to_all(summed, "head", split_axis=0, concat_axis=0, tiled=True)
    slices = (shape((32, 512), BF16),) * 4
    win_dk, win_dv, full_dk, full_dv, sink_grads = local_call(
        unpack_kernel, slices + (shape((2, 16), F32),), (grads, sink_terms)
    )
    return win_dq, win_dk, win_dv, full_dq, full_dk, full_dv, sink_grads


def solution(mesh):
    in_specs = (
        P("ctx", "head"),
        P(("ctx", "head"), None),
        P(("ctx", "head"), None),
        P("ctx", "head"),
        P("ctx", "head"),
        P(("ctx", "head"), None),
        P(("ctx", "head"), None),
        P("ctx", "head"),
        P(None, "head"),
        P(),
    )
    out_specs = (
        P("ctx", "head"),
        P(("ctx", "head"), None),
        P(("ctx", "head"), None),
        P("ctx", "head"),
        P(("ctx", "head"), None),
        P(("ctx", "head"), None),
        P(None, "head"),
    )
    return jax.shard_map(body, mesh=mesh, in_specs=in_specs, out_specs=out_specs, check_vma=False)
```

```python
import jax
import jax.numpy as jnp
from jax import lax
from jax.experimental import pallas as pl
from jax.experimental.pallas import tpu as pltpu
from jax.sharding import PartitionSpec as P

HEAD_DIM = 64
CYCLE = 4
BLOCK = 128
PAIRS = 4
NEG = -1e30
PAIRS_OF_BLOCKS = 64
CHUNK = 48
VMEM = pl.BlockSpec(memory_space=pltpu.VMEM)
SMEM = pl.BlockSpec(memory_space=pltpu.SMEM)
ANY = pl.BlockSpec(memory_space=pl.ANY)
HBM = pl.BlockSpec(memory_space=pltpu.HBM)
BF16, F32 = jnp.bfloat16, jnp.float32


def passed_along(shard, axis, by):
    size = lax.axis_size(axis)
    pairs = [(i, i + by) for i in range(size) if 0 <= i + by < size]
    return lax.ppermute(shard, axis, pairs)


def low_lanes(rows):
    return lax.broadcasted_iota(jnp.int32, (rows, 128), 1) < 64


def both_ways(tile):
    turned = pltpu.roll(tile, 64, 1)
    low = low_lanes(tile.shape[0])
    return jnp.where(low, tile, turned), jnp.where(low, turned, tile)


def pair_rows(tile):
    low = low_lanes(128)
    zero = jnp.zeros_like(tile)
    return jnp.concatenate([jnp.where(low, tile, zero), jnp.where(low, zero, tile)], axis=0)


def dot(a, b, contract):
    return lax.dot_general(a, b, (contract, ((), ())), preferred_element_type=F32)


def build_bias(bias, seg_ref, me, blocks, windowed):
    seg_q = jnp.broadcast_to(seg_ref[pl.ds(me, 1), :], (128, 128))
    key_row = lax.broadcasted_iota(jnp.int32, (128, 128), 0)
    query_col = lax.broadcasted_iota(jnp.int32, (128, 128), 1)
    for b in range(blocks):
        lag = blocks - 1 - b
        at = me - lag
        seg_row = jnp.broadcast_to(seg_ref[pl.ds(jnp.maximum(at, 0), 1), :], (128, 128))
        seg_k = jnp.transpose(seg_row.astype(F32)).astype(jnp.int32)
        allowed = (seg_k == seg_q) & (at >= 0)
        if lag == 0:
            allowed = allowed & (key_row <= query_col)
        elif windowed:
            allowed = allowed & (key_row > query_col)
        tile = jnp.where(allowed, 0.0, NEG).astype(F32)
        bias[b * 128 : (b + 1) * 128, :] = jnp.concatenate([tile, tile], axis=1)


def layer(layer_id, sinks_ref, q_ref, do_ref, odd, places, bias, kd, vd, kt, ws, dss, dq_ref, sink_acc, dq_hbm, sems):
    blocks = len(places) - 1
    rows = blocks * 128

    def block(b, shift):
        first, second = (
            ref[row : row + 128, col + shift : col + shift + 128].astype(F32) for ref, row, col in places[b : b + 2]
        )
        return jnp.where(odd, second, first)

    for b in range(blocks):
        span = slice(b * 128, (b + 1) * 128)
        key = block(b, 0) * (HEAD_DIM**-0.5)
        k0, k1 = both_ways(key)
        kd[0, span, :] = k0.astype(BF16)
        kd[1, span, :] = k1.astype(BF16)
        turned = jnp.transpose(key).astype(BF16)
        kt[0, :, span] = turned[:64]
        kt[1, :, span] = turned[64:]
        v0, v1 = both_ways(block(b, 128))
        vd[0, span, :] = v0.astype(BF16)
        vd[1, span, :] = v1.astype(BF16)
    lane = lax.broadcasted_iota(jnp.int32, (1, 256), 1)
    sums, sends = [], []
    for g in range(2):
        q2s, do2s = [], []
        for j in range(PAIRS):
            p = g * PAIRS + j
            q2 = pair_rows(q_ref[:, p * 128 : (p + 1) * 128])
            do2 = pair_rows(do_ref[:, p * 128 : (p + 1) * 128])
            q2s.append(q2)
            do2s.append(do2)
            sink = jnp.where(lane < 128, sinks_ref[layer_id : layer_id + 1, 2 * p : 2 * p + 1], sinks_ref[layer_id : layer_id + 1, 2 * p + 1 : 2 * p + 2])
            s = dot(kd[g, :rows, :], q2, ((1,), (1,))) + bias[:rows, :]
            m = jnp.maximum(jnp.max(s, axis=0, keepdims=True), sink)
            e = jnp.exp(s - m)
            sink_term = jnp.exp(sink - m)
            inverse = 1.0 / (jnp.sum(e, axis=0, keepdims=True) + sink_term)
            pr = e * inverse
            dp = dot(vd[g, :rows, :], do2, ((1,), (1,)))
            delta = jnp.sum(pr * dp, axis=0, keepdims=True)
            ws[:rows, j * 256 : (j + 1) * 256] = pr.astype(BF16)
            dss[:rows, j * 256 : (j + 1) * 256] = (pr * (dp - delta)).astype(BF16)
            grad = -(sink_term * inverse) * delta
            at = layer_id * 16 + 2 * p
            sink_acc[at : at + 1, :] = grad[:, :128]
            sink_acc[at + 1 : at + 2, :] = grad[:, 128:]
        q_all = jnp.concatenate(q2s, axis=0)
        do_all = jnp.concatenate(do2s, axis=0)
        dk = dot(dss[:rows, :], q_all, ((1,), (0,)))
        dv = dot(ws[:rows, :], do_all, ((1,), (0,)))
        sums.append((dk + pltpu.roll(dk, 64, 1), dv + pltpu.roll(dv, 64, 1)))
        dqt = dot(kt[g, :, :rows], dss[:rows, :], ((1,), (0,)))
        for j in range(PAIRS):
            p = g * PAIRS + j
            both = jnp.concatenate([dqt[:, j * 256 : j * 256 + 128], dqt[:, j * 256 + 128 : j * 256 + 256]], axis=0)
            dq_ref[:, p * 128 : (p + 1) * 128] = jnp.transpose(both).astype(BF16)
        cols = slice(g * 512, (g + 1) * 512)
        sends.append(pltpu.make_async_copy(dq_ref.at[:, cols], dq_hbm.at[:, cols], sems.at[1 + g]))
        sends[-1].start()
    low = low_lanes(rows)
    dk = jnp.where(low, sums[0][0], sums[1][0]) * (HEAD_DIM**-0.5)
    dv = jnp.where(low, sums[0][1], sums[1][1])
    for send in sends:
        send.wait()
    return dk, dv


def shifted(grad, blocks, odd):
    zero = jnp.zeros((128, 128), F32)
    parts = [zero] + [grad[b * 128 : (b + 1) * 128] for b in range(blocks)] + [zero]
    return [jnp.where(odd, parts[b], parts[b + 1]) for b in range(blocks + 1)]


def window_kernel(
    me_ref, sinks_hbm, seg_ref, q_ref, do_ref, own, far2,
    dq_hbm, mine, back, sinks_ref, band_bias, sink_acc,
    bias, kd, vd, kt, ws, dss, dq_ref, sems,
):
    me, odd = me_ref[0], me_ref[1] == 1
    fetch = pltpu.make_async_copy(sinks_hbm, sinks_ref, sems.at[0])
    fetch.start()
    sink_acc[...] = jnp.zeros_like(sink_acc)
    build_bias(bias, seg_ref, me, 2, True)
    build_bias(band_bias, seg_ref, me, CYCLE + 1, False)
    fetch.wait()
    blocks = [(far2, 256, 0), (own, 0, 0), (own, 128, 0)]
    dk, dv = layer(
        0, sinks_ref, q_ref, do_ref, odd, blocks, bias, kd, vd, kt, ws, dss, dq_ref, sink_acc, dq_hbm, sems
    )
    for at, grad in ((0, dk), (128, dv)):
        parts = shifted(grad, 2, odd)
        back[:, at : at + 128] = parts[0].astype(BF16)
        mine[:128, at : at + 128] = parts[1]
        mine[128:, at : at + 128] = parts[2]


def band_kernel(
    me_ref, sinks_ref, bias, q_ref, do_ref, own, far2, far4, win_back, win_acc,
    dq_hbm, mine, back2, back4, sink_ref,
    kd, vd, kt, ws, dss, dq_ref, sink_acc, sems,
):
    odd = me_ref[1] == 1
    sink_acc[...] = win_acc[...]
    blocks = [(far4, 0, 0), (far4, 128, 0), (far2, 0, 0), (far2, 128, 0), (own, 0, 256), (own, 128, 256)]
    dk, dv = layer(
        1, sinks_ref, q_ref, do_ref, odd, blocks, bias, kd, vd, kt, ws, dss, dq_ref, sink_acc, dq_hbm, sems
    )
    for at, grad in ((0, dk), (128, dv)):
        parts = shifted(grad, CYCLE + 1, odd)
        for half in range(2):
            rows = slice(half * 128, (half + 1) * 128)
            back4[rows, at : at + 128] = parts[half].astype(BF16)
            back2[rows, at : at + 128] = parts[2 + half].astype(BF16)
            mine[rows, at : at + 128] = parts[4 + half]
    back2[256:, :] = win_back[...]
    total = jnp.sum(jnp.transpose(sink_acc[...]), axis=0, keepdims=True)
    row = lax.broadcasted_iota(jnp.int32, sink_ref.shape, 0)
    sink_ref[...] = jnp.where(row % 2 == 0, total, 0.0)


def scratch(rows):
    return [
        pltpu.VMEM((2, rows, 128), BF16),
        pltpu.VMEM((2, rows, 128), BF16),
        pltpu.VMEM((2, 64, rows), BF16),
        pltpu.VMEM((rows, 1024), BF16),
        pltpu.VMEM((rows, 1024), BF16),
        pltpu.VMEM((128, 1024), BF16),
    ]


def window_call(me, sinks, seg, q, do, own, far2):
    shape = jax.ShapeDtypeStruct
    return pl.pallas_call(
        window_kernel,
        out_shape=(
            shape((128, 1024), BF16), shape((256, 256), F32), shape((128, 256), BF16),
            shape((2, 16), F32), shape(((CYCLE + 1) * 128, 256), F32), shape((128, 128), F32),
        ),
        in_specs=[SMEM, HBM] + [VMEM] * 5,
        out_specs=[HBM] + [VMEM] * 5,
        scratch_shapes=[pltpu.VMEM((256, 256), F32)] + scratch(256) + [pltpu.SemaphoreType.DMA((3,))],
        compiler_params=pltpu.CompilerParams(vmem_limit_bytes=14 << 20),
        cost_estimate=pl.CostEstimate(flops=2_000_000_000, bytes_accessed=1_000_000, transcendentals=500_000),
    )(me, sinks, seg, q, do, own, far2)


def band_call(me, sinks, bias, q, do, own, far2, far4, win_back, win_acc):
    shape = jax.ShapeDtypeStruct
    return pl.pallas_call(
        band_kernel,
        out_shape=(
            shape((128, 1024), BF16), shape((256, 256), F32), shape((384, 256), BF16), shape((256, 256), BF16),
            shape((PAIRS_OF_BLOCKS * 2, 128), F32),
        ),
        in_specs=[SMEM] + [VMEM] * 9,
        out_specs=[HBM] + [VMEM] * 4,
        scratch_shapes=scratch((CYCLE + 1) * 128) + [pltpu.VMEM((128, 128), F32), pltpu.SemaphoreType.DMA((3,))],
        compiler_params=pltpu.CompilerParams(vmem_limit_bytes=24 << 20),
        cost_estimate=pl.CostEstimate(flops=5_000_000_000, bytes_accessed=2_000_000, transcendentals=1_500_000),
    )(me, sinks, bias, q, do, own, far2, far4, win_back, win_acc)


def pack_kernel(wk, wv, fk, fv, out, held, sems):
    copies = [pltpu.make_async_copy(ref, held.at[a], sems.at[a]) for a, ref in enumerate((wk, wv, fk, fv))]
    for copy in copies:
        copy.start()
    for a, copy in enumerate(copies):
        copy.wait()
        for t in range(8):
            h = t % 4
            out[t * 32 : (t + 1) * 32, a * 128 : (a + 1) * 128] = held[a, :, h * 128 : (h + 1) * 128]


def three_parts(row):
    high = row.astype(BF16).astype(F32)
    middle = (row - high).astype(BF16).astype(F32)
    low = row - high - middle
    at = lax.broadcasted_iota(jnp.int32, (16, 128), 0)
    rest = jnp.where(at == 2, low, 0.0)
    return jnp.where(at == 0, high, jnp.where(at == 1, middle, rest)).astype(BF16)


def sum_kernel(win_mine, band_mine, back2, back4, sink_terms, out):
    win = [win_mine[:128, :], win_mine[128:, :] + back2[256:, :].astype(F32)]
    sinks = three_parts(jnp.sum(sink_terms[...], axis=0, keepdims=True))
    for half in range(2):
        rows = slice(half * 128, (half + 1) * 128)
        band = (band_mine[rows, :] + back2[rows, :].astype(F32) + back4[rows, :].astype(F32)).astype(BF16)
        for t in range(4):
            at = (half * 4 + t) * CHUNK
            out[at : at + 32, :256] = win[half][t * 32 : (t + 1) * 32].astype(BF16)
            out[at : at + 32, 256:] = band[t * 32 : (t + 1) * 32]
            out[at + 32 : at + 48, :128] = sinks
            out[at + 32 : at + 48, 128:] = jnp.zeros((16, 384), BF16)


def unpack_kernel(me_ref, grads, wk, wv, fk, fv, sinks):
    def chunk(yh, t):
        at = (yh * 4 + t) * CHUNK
        return grads[at : at + 32, :].astype(F32)

    for t in range(4):
        total = (chunk(0, t) + chunk(1, t)).astype(BF16)
        for a, ref in enumerate((wk, wv, fk, fv)):
            ref[:, t * 128 : (t + 1) * 128] = total[:, a * 128 : (a + 1) * 128]
    parts = jnp.zeros((16, 128), F32)
    for yh in range(2):
        at = pl.multiple_of((yh * 4 + me_ref[2]) * CHUNK + 32, 16)
        parts = parts + grads[pl.ds(at, 16), :128].astype(F32)
    total = jnp.sum(parts, axis=0, keepdims=True)
    sinks[0:1, :] = total[:, 0:16]
    sinks[1:2, :] = total[:, 16:32]


def local_call(kernel, out_shape, args, in_specs, scratch_shapes=(), flops=100_000, vmem=4):
    return pl.pallas_call(
        kernel,
        out_shape=out_shape,
        in_specs=in_specs,
        out_specs=jax.tree.map(lambda _: VMEM, out_shape),
        scratch_shapes=scratch_shapes,
        compiler_params=pltpu.CompilerParams(vmem_limit_bytes=vmem << 20),
        cost_estimate=pl.CostEstimate(flops=flops, bytes_accessed=500_000, transcendentals=0),
    )(*args)


def body(win_q, win_k, win_v, win_dout, full_q, full_k, full_v, full_dout, sinks, segments):
    shape = jax.ShapeDtypeStruct
    held = [pltpu.VMEM((4, 32, 512), BF16), pltpu.SemaphoreType.DMA((4,))]
    packed = local_call(pack_kernel, shape((256, 512), BF16), (win_k, win_v, full_k, full_v), [HBM] * 4, held, vmem=60)
    own = lax.all_to_all(packed, ("yh", "head"), split_axis=0, concat_axis=0, tiled=True)
    banded = own[:, 256:]
    far2 = passed_along(jnp.concatenate([banded, own[128:, :256]], axis=0), "pair", 1)
    far4 = passed_along(banded, "pair", 2)
    pair, yh, head = (lax.axis_index(axis).astype(jnp.int32) for axis in ("pair", "yh", "head"))
    me = jnp.stack([pair * 2 + yh, yh, head])
    win_dq, win_mine, win_back, sink_vals, bias, win_acc = window_call(
        me, sinks, segments.reshape(128, 128), win_q, win_dout, own, far2
    )
    full_dq, band_mine, back2, back4, sink_rows = band_call(
        me, sink_vals, bias, full_q, full_dout, own, far2, far4, win_back, win_acc
    )
    back2, back4 = passed_along(back2, "pair", -1), passed_along(back4, "pair", -2)
    sink_terms = lax.all_to_all(sink_rows, "pair", split_axis=0, concat_axis=0, tiled=True)
    summed = local_call(
        sum_kernel, shape((8 * CHUNK, 512), BF16), (win_mine, band_mine, back2, back4, sink_terms), [VMEM] * 5
    )
    grads = lax.all_to_all(summed, ("yh", "head"), split_axis=0, concat_axis=0, tiled=True)
    win_dk, win_dv, full_dk, full_dv, sink_grads = local_call(
        unpack_kernel, (shape((32, 512), BF16),) * 4 + (shape((2, 16), F32),), (me, grads), [SMEM, VMEM]
    )
    return win_dq, win_dk, win_dv, full_dq, full_dk, full_dv, sink_grads


def solution(mesh):
    mesh = jax.sharding.Mesh(mesh.devices.reshape(PAIRS_OF_BLOCKS, 2, 4), ("pair", "yh", "head"))
    tokens = P(("pair", "yh"), "head")
    slices = P(("pair", "yh", "head"), None)
    in_specs = (tokens, slices, slices, tokens, tokens, slices, slices, tokens, P(None, "head"), P())
    out_specs = (tokens, slices, slices, tokens, slices, slices, P(None, "head"))
    return jax.shard_map(body, mesh=mesh, in_specs=in_specs, out_specs=out_specs, check_vma=False)
```

```python
import jax
import jax.numpy as jnp
from jax import lax
from jax.experimental import pallas as pl
from jax.experimental.pallas import tpu as pltpu
from jax.sharding import PartitionSpec as P

HEAD_DIM = 64
CYCLE = 4
BLOCK = 128
PAIRS = 4
NEG = -1e30
PAIRS_OF_BLOCKS = 64
VMEM = pl.BlockSpec(memory_space=pltpu.VMEM)
SMEM = pl.BlockSpec(memory_space=pltpu.SMEM)
ANY = pl.BlockSpec(memory_space=pl.ANY)
HBM = pl.BlockSpec(memory_space=pltpu.HBM)
BF16, F32 = jnp.bfloat16, jnp.float32


def passed_along(shard, axis, by):
    size = lax.axis_size(axis)
    pairs = [(i, i + by) for i in range(size) if 0 <= i + by < size]
    return lax.ppermute(shard, axis, pairs)


def low_lanes(rows):
    return lax.broadcasted_iota(jnp.int32, (rows, 128), 1) < 64


def both_ways(tile):
    turned = pltpu.roll(tile, 64, 1)
    low = low_lanes(tile.shape[0])
    return jnp.where(low, tile, turned), jnp.where(low, turned, tile)


def pair_rows(tile):
    low = low_lanes(128)
    zero = jnp.zeros_like(tile)
    return jnp.concatenate([jnp.where(low, tile, zero), jnp.where(low, zero, tile)], axis=0)


def dot(a, b, contract):
    return lax.dot_general(a, b, (contract, ((), ())), preferred_element_type=F32)


def build_bias(bias, seg_ref, me, blocks, windowed):
    seg_q = jnp.broadcast_to(seg_ref[pl.ds(me, 1), :], (128, 128))
    key_row = lax.broadcasted_iota(jnp.int32, (128, 128), 0)
    query_col = lax.broadcasted_iota(jnp.int32, (128, 128), 1)
    for b in range(blocks):
        lag = blocks - 1 - b
        at = me - lag
        seg_row = jnp.broadcast_to(seg_ref[pl.ds(jnp.maximum(at, 0), 1), :], (128, 128))
        seg_k = jnp.transpose(seg_row.astype(F32)).astype(jnp.int32)
        allowed = (seg_k == seg_q) & (at >= 0)
        if lag == 0:
            allowed = allowed & (key_row <= query_col)
        elif windowed:
            allowed = allowed & (key_row > query_col)
        tile = jnp.where(allowed, 0.0, NEG).astype(F32)
        bias[b * 128 : (b + 1) * 128, :] = jnp.concatenate([tile, tile], axis=1)


def layer(layer_id, sinks_ref, q_ref, do_ref, odd, places, bias, kd, vd, kt, ws, dss, dq_ref, sink_acc, sends=(), send_sinks=None):
    blocks = len(places) - 1
    rows = blocks * 128

    def block(b, shift):
        first, second = (
            ref[row : row + 128, col + shift : col + shift + 128].astype(F32) for ref, row, col in places[b : b + 2]
        )
        return jnp.where(odd, second, first)

    for b in range(blocks):
        span = slice(b * 128, (b + 1) * 128)
        key = block(b, 0) * (HEAD_DIM**-0.5)
        k0, k1 = both_ways(key)
        kd[0, span, :] = k0.astype(BF16)
        kd[1, span, :] = k1.astype(BF16)
        turned = jnp.transpose(key).astype(BF16)
        kt[0, :, span] = turned[:64]
        kt[1, :, span] = turned[64:]
        v0, v1 = both_ways(block(b, 128))
        vd[0, span, :] = v0.astype(BF16)
        vd[1, span, :] = v1.astype(BF16)
    lane = lax.broadcasted_iota(jnp.int32, (1, 256), 1)
    sums = []
    for g in range(2):
        q2s, do2s = [], []
        for j in range(PAIRS):
            p = g * PAIRS + j
            q2 = pair_rows(q_ref[:, p * 128 : (p + 1) * 128])
            do2 = pair_rows(do_ref[:, p * 128 : (p + 1) * 128])
            q2s.append(q2)
            do2s.append(do2)
            sink = jnp.where(lane < 128, sinks_ref[layer_id : layer_id + 1, 2 * p : 2 * p + 1], sinks_ref[layer_id : layer_id + 1, 2 * p + 1 : 2 * p + 2])
            s = dot(kd[g, :rows, :], q2, ((1,), (1,))) + bias[:rows, :]
            m = jnp.maximum(jnp.max(s, axis=0, keepdims=True), sink)
            e = jnp.exp(s - m)
            sink_term = jnp.exp(sink - m)
            inverse = 1.0 / (jnp.sum(e, axis=0, keepdims=True) + sink_term)
            pr = e * inverse
            dp = dot(vd[g, :rows, :], do2, ((1,), (1,)))
            delta = jnp.sum(pr * dp, axis=0, keepdims=True)
            ws[:rows, j * 256 : (j + 1) * 256] = pr.astype(BF16)
            dss[:rows, j * 256 : (j + 1) * 256] = (pr * (dp - delta)).astype(BF16)
            grad = -(sink_term * inverse) * delta
            at = layer_id * 16 + 2 * p
            sink_acc[at : at + 1, :] = grad[:, :128]
            sink_acc[at + 1 : at + 2, :] = grad[:, 128:]
        if g == 1 and send_sinks is not None:
            send_sinks()
        q_all = jnp.concatenate(q2s, axis=0)
        do_all = jnp.concatenate(do2s, axis=0)
        dqt = dot(kt[g, :, :rows], dss[:rows, :], ((1,), (0,)))
        for j in range(PAIRS):
            p = g * PAIRS + j
            both = jnp.concatenate([dqt[:, j * 256 : j * 256 + 128], dqt[:, j * 256 + 128 : j * 256 + 256]], axis=0)
            dq_ref[:, p * 128 : (p + 1) * 128] = jnp.transpose(both).astype(BF16)
        if sends:
            sends[g].start()
        dk = dot(dss[:rows, :], q_all, ((1,), (0,)))
        dv = dot(ws[:rows, :], do_all, ((1,), (0,)))
        sums.append((dk + pltpu.roll(dk, 64, 1), dv + pltpu.roll(dv, 64, 1)))
    low = low_lanes(rows)
    dk = jnp.where(low, sums[0][0], sums[1][0]) * (HEAD_DIM**-0.5)
    dv = jnp.where(low, sums[0][1], sums[1][1])
    return dk, dv


def shifted(grad, blocks, odd):
    zero = jnp.zeros((128, 128), F32)
    parts = [zero] + [grad[b * 128 : (b + 1) * 128] for b in range(blocks)] + [zero]
    return [jnp.where(odd, parts[b], parts[b + 1]) for b in range(blocks + 1)]


def window_kernel(
    sinks_hbm, seg_ref, q_ref, do_ref, own, far2,
    dq_ref, mine, back, sinks_ref, band_bias, sink_acc,
    bias, kd, vd, kt, ws, dss, sems,
):
    odd = lax.axis_index("yh") == 1
    me = lax.axis_index("pair") * 2 + lax.axis_index("yh")
    fetch = pltpu.make_async_copy(sinks_hbm, sinks_ref, sems.at[0])
    fetch.start()
    sink_acc[...] = jnp.zeros_like(sink_acc)
    build_bias(bias, seg_ref, me, 2, True)
    build_bias(band_bias, seg_ref, me, CYCLE + 1, False)
    fetch.wait()
    blocks = [(far2, 256, 0), (own, 0, 0), (own, 128, 0)]
    dk, dv = layer(
        0, sinks_ref, q_ref, do_ref, odd, blocks, bias, kd, vd, kt, ws, dss, dq_ref, sink_acc
    )
    for at, grad in ((0, dk), (128, dv)):
        parts = shifted(grad, 2, odd)
        back[:, at : at + 128] = parts[0].astype(BF16)
        mine[:128, at : at + 128] = parts[1]
        mine[128:, at : at + 128] = parts[2]


def band_kernel(
    sinks_ref, bias, q_ref, do_ref, own, far2, far4, win_back, win_acc, win_dq,
    win_dq_hbm, dq_hbm, mine, back2, back4, sink_hbm,
    kd, vd, kt, ws, dss, dq_ref, sink_acc, sink_ref, sems,
):
    odd = lax.axis_index("yh") == 1
    win_send = pltpu.make_async_copy(win_dq, win_dq_hbm, sems.at[0])
    win_send.start()
    sink_acc[...] = win_acc[...]
    blocks = [(far4, 0, 0), (far4, 128, 0), (far2, 0, 0), (far2, 128, 0), (own, 0, 256), (own, 128, 256)]
    halves = (slice(0, 512), slice(512, 1024))
    sends = [
        pltpu.make_async_copy(dq_ref.at[:, cols], dq_hbm.at[:, cols], sems.at[1 + g]) for g, cols in enumerate(halves)
    ]
    sink_send = pltpu.make_async_copy(sink_ref, sink_hbm, sems.at[3])

    def send_sinks():
        total = jnp.sum(jnp.transpose(sink_acc[...]), axis=0, keepdims=True)
        row = lax.broadcasted_iota(jnp.int32, sink_ref.shape, 0)
        sink_ref[...] = jnp.where(row % 2 == 0, total, 0.0)
        sink_send.start()

    dk, dv = layer(
        1, sinks_ref, q_ref, do_ref, odd, blocks, bias, kd, vd, kt, ws, dss, dq_ref, sink_acc, sends, send_sinks
    )
    for at, grad in ((0, dk), (128, dv)):
        parts = shifted(grad, CYCLE + 1, odd)
        for half in range(2):
            rows = slice(half * 128, (half + 1) * 128)
            back4[rows, at : at + 128] = parts[half].astype(BF16)
            back2[rows, at : at + 128] = parts[2 + half].astype(BF16)
            mine[rows, at : at + 128] = parts[4 + half]
    back2[256:, :] = win_back[...]
    for send in [win_send, sink_send] + sends:
        send.wait()


def scratch(rows):
    return [
        pltpu.VMEM((2, rows, 128), BF16),
        pltpu.VMEM((2, rows, 128), BF16),
        pltpu.VMEM((2, 64, rows), BF16),
        pltpu.VMEM((rows, 1024), BF16),
        pltpu.VMEM((rows, 1024), BF16),
        pltpu.VMEM((128, 1024), BF16),
    ]


def window_call(sinks, seg, q, do, own, far2):
    shape = jax.ShapeDtypeStruct
    return pl.pallas_call(
        window_kernel,
        out_shape=(
            shape((128, 1024), BF16), shape((256, 256), F32), shape((128, 256), BF16),
            shape((2, 16), F32), shape(((CYCLE + 1) * 128, 256), F32), shape((128, 128), F32),
        ),
        in_specs=[HBM] + [VMEM] * 5,
        out_specs=[VMEM] * 6,
        scratch_shapes=[pltpu.VMEM((256, 256), F32)] + scratch(256)[:-1] + [pltpu.SemaphoreType.DMA((1,))],
        compiler_params=pltpu.CompilerParams(vmem_limit_bytes=14 << 20),
        cost_estimate=pl.CostEstimate(flops=2_000_000_000, bytes_accessed=1_000_000, transcendentals=500_000),
    )(sinks, seg, q, do, own, far2)


def band_call(sinks, bias, q, do, own, far2, far4, win_back, win_acc, win_dq):
    shape = jax.ShapeDtypeStruct
    return pl.pallas_call(
        band_kernel,
        out_shape=(
            shape((128, 1024), BF16), shape((128, 1024), BF16),
            shape((256, 256), F32), shape((384, 256), BF16), shape((256, 256), BF16),
            shape((PAIRS_OF_BLOCKS * 2, 128), F32),
        ),
        in_specs=[VMEM] * 10,
        out_specs=[HBM] * 2 + [VMEM] * 3 + [HBM],
        scratch_shapes=scratch((CYCLE + 1) * 128) + [pltpu.VMEM((128, 128), F32)] * 2 + [pltpu.SemaphoreType.DMA((4,))],
        compiler_params=pltpu.CompilerParams(vmem_limit_bytes=24 << 20),
        cost_estimate=pl.CostEstimate(flops=5_000_000_000, bytes_accessed=2_000_000, transcendentals=1_500_000),
    )(sinks, bias, q, do, own, far2, far4, win_back, win_acc, win_dq)


def pack_kernel(wk, wv, fk, fv, out, held, sems):
    copies = [pltpu.make_async_copy(ref, held.at[a], sems.at[a]) for a, ref in enumerate((wk, wv, fk, fv))]
    for copy in copies:
        copy.start()
    for a, copy in enumerate(copies):
        copy.wait()
        for t in range(8):
            h = t % 4
            out[t * 32 : (t + 1) * 32, a * 128 : (a + 1) * 128] = held[a, :, h * 128 : (h + 1) * 128]


def three_parts(row):
    high = row.astype(BF16).astype(F32)
    middle = (row - high).astype(BF16).astype(F32)
    low = row - high - middle
    at = lax.broadcasted_iota(jnp.int32, (16, 128), 0)
    rest = jnp.where(at == 2, low, 0.0)
    return jnp.where(at == 0, high, jnp.where(at == 1, middle, rest)).astype(BF16)


def sum_kernel(win_mine, band_mine, back2, back4, sink_terms, out):
    win = [win_mine[:128, :], win_mine[128:, :] + back2[256:, :].astype(F32)]
    sinks = three_parts(jnp.sum(sink_terms[...], axis=0, keepdims=True))
    for half in range(2):
        rows = slice(half * 128, (half + 1) * 128)
        band = (band_mine[rows, :] + back2[rows, :].astype(F32) + back4[rows, :].astype(F32)).astype(BF16)
        for t in range(4):
            at = (half * 4 + t) * 32
            out[at : at + 32, :256] = win[half][t * 32 : (t + 1) * 32].astype(BF16)
            out[at : at + 32, 256:512] = band[t * 32 : (t + 1) * 32]
            out[at : at + 16, 512:] = sinks
            out[at + 16 : at + 32, 512:] = jnp.zeros((16, 128), BF16)


def unpack_kernel(grads, wk, wv, fk, fv, sinks):
    def chunk(yh, t):
        at = (yh * 4 + t) * 32
        return grads[at : at + 32, :512].astype(F32)

    for t in range(4):
        total = (chunk(0, t) + chunk(1, t)).astype(BF16)
        for a, ref in enumerate((wk, wv, fk, fv)):
            ref[:, t * 128 : (t + 1) * 128] = total[:, a * 128 : (a + 1) * 128]
    parts = jnp.zeros((16, 128), F32)
    for yh in range(2):
        at = pl.multiple_of((yh * 4 + lax.axis_index("head")) * 32, 32)
        parts = parts + grads[pl.ds(at, 16), 512:].astype(F32)
    total = jnp.sum(parts, axis=0, keepdims=True)
    sinks[0:1, :] = total[:, 0:16]
    sinks[1:2, :] = total[:, 16:32]


def local_call(kernel, out_shape, args, in_specs, scratch_shapes=(), flops=100_000, vmem=4):
    return pl.pallas_call(
        kernel,
        out_shape=out_shape,
        in_specs=in_specs,
        out_specs=jax.tree.map(lambda _: VMEM, out_shape),
        scratch_shapes=scratch_shapes,
        compiler_params=pltpu.CompilerParams(vmem_limit_bytes=vmem << 20),
        cost_estimate=pl.CostEstimate(flops=flops, bytes_accessed=500_000, transcendentals=0),
    )(*args)


def body(win_q, win_k, win_v, win_dout, full_q, full_k, full_v, full_dout, sinks, segments):
    shape = jax.ShapeDtypeStruct
    held = [pltpu.VMEM((4, 32, 512), BF16), pltpu.SemaphoreType.DMA((4,))]
    packed = local_call(pack_kernel, shape((256, 512), BF16), (win_k, win_v, full_k, full_v), [HBM] * 4, held, vmem=60)
    own = lax.all_to_all(packed, ("yh", "head"), split_axis=0, concat_axis=0, tiled=True)
    banded = own[:, 256:]
    far2 = passed_along(jnp.concatenate([banded, own[128:, :256]], axis=0), "pair", 1)
    far4 = passed_along(banded, "pair", 2)
    win_dq, win_mine, win_back, sink_vals, bias, win_acc = window_call(
        sinks, segments.reshape(128, 128), win_q, win_dout, own, far2
    )
    win_dq, full_dq, band_mine, back2, back4, sink_rows = band_call(
        sink_vals, bias, full_q, full_dout, own, far2, far4, win_back, win_acc, win_dq
    )
    back2, back4 = passed_along(back2, "pair", -1), passed_along(back4, "pair", -2)
    sink_terms = lax.all_to_all(sink_rows, "pair", split_axis=0, concat_axis=0, tiled=True)
    summed = local_call(
        sum_kernel, shape((256, 640), BF16), (win_mine, band_mine, back2, back4, sink_terms), [VMEM] * 5
    )
    grads = lax.all_to_all(summed, ("yh", "head"), split_axis=0, concat_axis=0, tiled=True)
    win_dk, win_dv, full_dk, full_dv, sink_grads = local_call(
        unpack_kernel, (shape((32, 512), BF16),) * 4 + (shape((2, 16), F32),), (grads,), [VMEM]
    )
    return win_dq, win_dk, win_dv, full_dq, full_dk, full_dv, sink_grads


def solution(mesh):
    mesh = jax.sharding.Mesh(mesh.devices.reshape(PAIRS_OF_BLOCKS, 2, 4), ("pair", "yh", "head"))
    tokens = P(("pair", "yh"), "head")
    slices = P(("pair", "yh", "head"), None)
    in_specs = (tokens, slices, slices, tokens, tokens, slices, slices, tokens, P(None, "head"), P())
    out_specs = (tokens, slices, slices, tokens, slices, slices, P(None, "head"))
    return jax.shard_map(body, mesh=mesh, in_specs=in_specs, out_specs=out_specs, check_vma=False)
```

```python
import jax
import jax.numpy as jnp
from jax import lax
from jax.experimental import pallas as pl
from jax.experimental.pallas import tpu as pltpu
from jax.sharding import PartitionSpec as P

HEAD_DIM = 64
CYCLE = 4
BLOCK = 128
PAIRS = 4
NEG = -1e30
PAIRS_OF_BLOCKS = 64
VMEM = pl.BlockSpec(memory_space=pltpu.VMEM)
SMEM = pl.BlockSpec(memory_space=pltpu.SMEM)
ANY = pl.BlockSpec(memory_space=pl.ANY)
HBM = pl.BlockSpec(memory_space=pltpu.HBM)
BF16, F32 = jnp.bfloat16, jnp.float32


def passed_along(shard, axis, by):
    size = lax.axis_size(axis)
    pairs = [(i, i + by) for i in range(size) if 0 <= i + by < size]
    return lax.ppermute(shard, axis, pairs)


def low_lanes(rows):
    return lax.broadcasted_iota(jnp.int32, (rows, 128), 1) < 64


def both_ways(tile):
    turned = pltpu.roll(tile, 64, 1)
    low = low_lanes(tile.shape[0])
    return jnp.where(low, tile, turned), jnp.where(low, turned, tile)


def pair_rows(tile):
    low = low_lanes(128)
    zero = jnp.zeros_like(tile)
    return jnp.concatenate([jnp.where(low, tile, zero), jnp.where(low, zero, tile)], axis=0)


def dot(a, b, contract):
    return lax.dot_general(a, b, (contract, ((), ())), preferred_element_type=F32)


def build_bias(bias, seg_ref, me, blocks, windowed):
    seg_q = jnp.broadcast_to(seg_ref[pl.ds(me, 1), :], (128, 128))
    key_row = lax.broadcasted_iota(jnp.int32, (128, 128), 0)
    query_col = lax.broadcasted_iota(jnp.int32, (128, 128), 1)
    for b in range(blocks):
        lag = blocks - 1 - b
        at = me - lag
        seg_row = jnp.broadcast_to(seg_ref[pl.ds(jnp.maximum(at, 0), 1), :], (128, 128))
        seg_k = jnp.transpose(seg_row.astype(F32)).astype(jnp.int32)
        allowed = (seg_k == seg_q) & (at >= 0)
        if lag == 0:
            allowed = allowed & (key_row <= query_col)
        elif windowed:
            allowed = allowed & (key_row > query_col)
        tile = jnp.where(allowed, 0.0, NEG).astype(F32)
        bias[b * 128 : (b + 1) * 128, :] = jnp.concatenate([tile, tile], axis=1)


def layer(layer_id, sinks_ref, q_ref, do_ref, odd, places, bias, kd, vd, kt, ws, dss, dq_ref, sink_acc, sends=(), send_sinks=None):
    blocks = len(places) - 1
    rows = blocks * 128

    def block(b, shift):
        first, second = (
            ref[row : row + 128, col + shift : col + shift + 128].astype(F32) for ref, row, col in places[b : b + 2]
        )
        return jnp.where(odd, second, first)

    for b in range(blocks):
        span = slice(b * 128, (b + 1) * 128)
        key = block(b, 0) * (HEAD_DIM**-0.5)
        k0, k1 = both_ways(key)
        kd[0, span, :] = k0.astype(BF16)
        kd[1, span, :] = k1.astype(BF16)
        turned = jnp.transpose(key).astype(BF16)
        kt[0, :, span] = turned[:64]
        kt[1, :, span] = turned[64:]
        v0, v1 = both_ways(block(b, 128))
        vd[0, span, :] = v0.astype(BF16)
        vd[1, span, :] = v1.astype(BF16)
    lane = lax.broadcasted_iota(jnp.int32, (1, 256), 1)
    sums = []
    for g in range(2):
        q2s, do2s = [], []
        for j in range(PAIRS):
            p = g * PAIRS + j
            q2 = pair_rows(q_ref[:, p * 128 : (p + 1) * 128])
            do2 = pair_rows(do_ref[:, p * 128 : (p + 1) * 128])
            q2s.append(q2)
            do2s.append(do2)
            sink = jnp.where(lane < 128, sinks_ref[layer_id : layer_id + 1, 2 * p : 2 * p + 1], sinks_ref[layer_id : layer_id + 1, 2 * p + 1 : 2 * p + 2])
            s = dot(kd[g, :rows, :], q2, ((1,), (1,))) + bias[:rows, :]
            m = jnp.maximum(jnp.max(s, axis=0, keepdims=True), sink)
            e = jnp.exp(s - m)
            sink_term = jnp.exp(sink - m)
            inverse = 1.0 / (jnp.sum(e, axis=0, keepdims=True) + sink_term)
            pr = e * inverse
            dp = dot(vd[g, :rows, :], do2, ((1,), (1,)))
            delta = jnp.sum(pr * dp, axis=0, keepdims=True)
            ws[:rows, j * 256 : (j + 1) * 256] = pr.astype(BF16)
            dss[:rows, j * 256 : (j + 1) * 256] = (pr * (dp - delta)).astype(BF16)
            grad = -(sink_term * inverse) * delta
            at = layer_id * 16 + 2 * p
            sink_acc[at : at + 1, :] = grad[:, :128]
            sink_acc[at + 1 : at + 2, :] = grad[:, 128:]
        if g == 1 and send_sinks is not None:
            send_sinks()
        q_all = jnp.concatenate(q2s, axis=0)
        do_all = jnp.concatenate(do2s, axis=0)
        dqt = dot(kt[g, :, :rows], dss[:rows, :], ((1,), (0,)))
        for j in range(PAIRS):
            p = g * PAIRS + j
            both = jnp.concatenate([dqt[:, j * 256 : j * 256 + 128], dqt[:, j * 256 + 128 : j * 256 + 256]], axis=0)
            dq_ref[:, p * 128 : (p + 1) * 128] = jnp.transpose(both).astype(BF16)
        if sends:
            sends[g].start()
        dk = dot(dss[:rows, :], q_all, ((1,), (0,)))
        dv = dot(ws[:rows, :], do_all, ((1,), (0,)))
        sums.append((dk + pltpu.roll(dk, 64, 1), dv + pltpu.roll(dv, 64, 1)))
    low = low_lanes(rows)
    dk = jnp.where(low, sums[0][0], sums[1][0]) * (HEAD_DIM**-0.5)
    dv = jnp.where(low, sums[0][1], sums[1][1])
    return dk, dv


def shifted(grad, blocks, odd):
    zero = jnp.zeros((128, 128), F32)
    parts = [zero] + [grad[b * 128 : (b + 1) * 128] for b in range(blocks)] + [zero]
    return [jnp.where(odd, parts[b], parts[b + 1]) for b in range(blocks + 1)]


def window_kernel(
    sinks_hbm, seg_ref, q_ref, do_ref, own, far2,
    dq_ref, mine, back, sinks_ref, band_bias, sink_acc,
    bias, kd, vd, kt, ws, dss, sems,
):
    odd = lax.axis_index("yh") == 1
    me = lax.axis_index("pair") * 2 + lax.axis_index("yh")
    fetch = pltpu.make_async_copy(sinks_hbm, sinks_ref, sems.at[0])
    fetch.start()
    sink_acc[...] = jnp.zeros_like(sink_acc)
    build_bias(bias, seg_ref, me, 2, True)
    build_bias(band_bias, seg_ref, me, CYCLE + 1, False)
    fetch.wait()
    blocks = [(far2, 256, 0), (own, 0, 0), (own, 128, 0)]
    dk, dv = layer(
        0, sinks_ref, q_ref, do_ref, odd, blocks, bias, kd, vd, kt, ws, dss, dq_ref, sink_acc
    )
    for at, grad in ((0, dk), (128, dv)):
        parts = shifted(grad, 2, odd)
        back[:, at : at + 128] = parts[0].astype(BF16)
        mine[:128, at : at + 128] = parts[1]
        mine[128:, at : at + 128] = parts[2]


def band_kernel(
    sinks_ref, bias, q_ref, do_ref, own, far2, far4, win_back, win_acc, win_dq,
    win_dq_hbm, dq_hbm, mine, back2, back4, sink_hbm,
    kd, vd, kt, ws, dss, dq_ref, sink_acc, sink_ref, sems,
):
    odd = lax.axis_index("yh") == 1
    win_send = pltpu.make_async_copy(win_dq, win_dq_hbm, sems.at[0])
    win_send.start()
    sink_acc[...] = win_acc[...]
    blocks = [(far4, 0, 0), (far4, 128, 0), (far2, 0, 0), (far2, 128, 0), (own, 0, 256), (own, 128, 256)]
    halves = (slice(0, 512), slice(512, 1024))
    sends = [
        pltpu.make_async_copy(dq_ref.at[:, cols], dq_hbm.at[:, cols], sems.at[1 + g]) for g, cols in enumerate(halves)
    ]
    sink_send = pltpu.make_async_copy(sink_ref, sink_hbm, sems.at[3])

    def send_sinks():
        total = jnp.sum(jnp.transpose(sink_acc[...]), axis=0, keepdims=True)
        row = lax.broadcasted_iota(jnp.int32, sink_ref.shape, 0)
        sink_ref[...] = jnp.where(row % 2 == 0, total, 0.0)
        sink_send.start()

    dk, dv = layer(
        1, sinks_ref, q_ref, do_ref, odd, blocks, bias, kd, vd, kt, ws, dss, dq_ref, sink_acc, sends, send_sinks
    )
    for at, grad in ((0, dk), (128, dv)):
        parts = shifted(grad, CYCLE + 1, odd)
        for half in range(2):
            rows = slice(half * 128, (half + 1) * 128)
            back4[rows, at : at + 128] = parts[half].astype(BF16)
            back2[rows, at : at + 128] = parts[2 + half].astype(BF16)
            mine[rows, at : at + 128] = parts[4 + half]
    back2[256:, :] = win_back[...]
    for send in [win_send, sink_send] + sends:
        send.wait()


def scratch(rows):
    return [
        pltpu.VMEM((2, rows, 128), BF16),
        pltpu.VMEM((2, rows, 128), BF16),
        pltpu.VMEM((2, 64, rows), BF16),
        pltpu.VMEM((rows, 1024), BF16),
        pltpu.VMEM((rows, 1024), BF16),
        pltpu.VMEM((128, 1024), BF16),
    ]


def window_call(sinks, seg, q, do, own, far2):
    shape = jax.ShapeDtypeStruct
    return pl.pallas_call(
        window_kernel,
        out_shape=(
            shape((128, 1024), BF16), shape((256, 256), F32), shape((128, 256), BF16),
            shape((2, 16), F32), shape(((CYCLE + 1) * 128, 256), F32), shape((128, 128), F32),
        ),
        in_specs=[HBM] + [VMEM] * 5,
        out_specs=[VMEM] * 6,
        scratch_shapes=[pltpu.VMEM((256, 256), F32)] + scratch(256)[:-1] + [pltpu.SemaphoreType.DMA((1,))],
        compiler_params=pltpu.CompilerParams(vmem_limit_bytes=14 << 20),
        cost_estimate=pl.CostEstimate(flops=2_000_000_000, bytes_accessed=1_000_000, transcendentals=500_000),
    )(sinks, seg, q, do, own, far2)


def band_call(sinks, bias, q, do, own, far2, far4, win_back, win_acc, win_dq):
    shape = jax.ShapeDtypeStruct
    return pl.pallas_call(
        band_kernel,
        out_shape=(
            shape((128, 1024), BF16), shape((128, 1024), BF16),
            shape((256, 256), F32), shape((384, 256), BF16), shape((256, 256), BF16),
            shape((PAIRS_OF_BLOCKS * 2, 128), F32),
        ),
        in_specs=[VMEM] * 10,
        out_specs=[HBM] * 2 + [VMEM] * 3 + [HBM],
        scratch_shapes=scratch((CYCLE + 1) * 128) + [pltpu.VMEM((128, 128), F32)] * 2 + [pltpu.SemaphoreType.DMA((4,))],
        compiler_params=pltpu.CompilerParams(vmem_limit_bytes=24 << 20),
        cost_estimate=pl.CostEstimate(flops=5_000_000_000, bytes_accessed=2_000_000, transcendentals=1_500_000),
    )(sinks, bias, q, do, own, far2, far4, win_back, win_acc, win_dq)


def pack_kernel(wk, wv, fk, fv, out, held, sems):
    copies = [pltpu.make_async_copy(ref, held.at[a], sems.at[a]) for a, ref in enumerate((wk, wv, fk, fv))]
    for copy in copies:
        copy.start()
    for a, copy in enumerate(copies):
        copy.wait()
        for t in range(8):
            h = t % 4
            out[t * 32 : (t + 1) * 32, a * 128 : (a + 1) * 128] = held[a, :, h * 128 : (h + 1) * 128]


def three_parts(row):
    high = row.astype(BF16).astype(F32)
    middle = (row - high).astype(BF16).astype(F32)
    low = row - high - middle
    at = lax.broadcasted_iota(jnp.int32, (16, 128), 0)
    rest = jnp.where(at == 2, low, 0.0)
    return jnp.where(at == 0, high, jnp.where(at == 1, middle, rest)).astype(BF16)


def sum_kernel(win_mine, band_mine, back2, back4, sink_terms, out):
    win = [win_mine[:128, :], win_mine[128:, :] + back2[256:, :].astype(F32)]
    sinks = three_parts(jnp.sum(sink_terms[...], axis=0, keepdims=True))
    for half in range(2):
        rows = slice(half * 128, (half + 1) * 128)
        band = (band_mine[rows, :] + back2[rows, :].astype(F32) + back4[rows, :].astype(F32)).astype(BF16)
        for t in range(4):
            at = (half * 4 + t) * 32
            out[at : at + 32, :256] = win[half][t * 32 : (t + 1) * 32].astype(BF16)
            out[at : at + 32, 256:512] = band[t * 32 : (t + 1) * 32]
            out[at : at + 16, 512:] = sinks
            out[at + 16 : at + 32, 512:] = jnp.zeros((16, 128), BF16)


def unpack_kernel(grads, wk, wv, fk, fv, sinks):
    def chunk(yh, t):
        at = (yh * 4 + t) * 32
        return grads[at : at + 32, :512].astype(F32)

    for t in range(4):
        total = (chunk(0, t) + chunk(1, t)).astype(BF16)
        for a, ref in enumerate((wk, wv, fk, fv)):
            ref[:, t * 128 : (t + 1) * 128] = total[:, a * 128 : (a + 1) * 128]
    parts = jnp.zeros((16, 128), F32)
    for yh in range(2):
        at = pl.multiple_of((yh * 4 + lax.axis_index("head")) * 32, 32)
        parts = parts + grads[pl.ds(at, 16), 512:].astype(F32)
    total = jnp.sum(parts, axis=0, keepdims=True)
    sinks[0:1, :] = total[:, 0:16]
    sinks[1:2, :] = total[:, 16:32]


def local_call(kernel, out_shape, args, in_specs, scratch_shapes=(), flops=100_000, vmem=4):
    return pl.pallas_call(
        kernel,
        out_shape=out_shape,
        in_specs=in_specs,
        out_specs=jax.tree.map(lambda _: VMEM, out_shape),
        scratch_shapes=scratch_shapes,
        compiler_params=pltpu.CompilerParams(vmem_limit_bytes=vmem << 20),
        cost_estimate=pl.CostEstimate(flops=flops, bytes_accessed=500_000, transcendentals=0),
    )(*args)


def body(win_q, win_k, win_v, win_dout, full_q, full_k, full_v, full_dout, sinks, segments):
    shape = jax.ShapeDtypeStruct
    held = [pltpu.VMEM((4, 32, 512), BF16), pltpu.SemaphoreType.DMA((4,))]
    packed = local_call(pack_kernel, shape((256, 512), BF16), [pltpu.with_memory_space_constraint(x, pltpu.HBM) for x in (win_k, win_v, full_k, full_v)], [HBM] * 4, held)
    own = lax.all_to_all(packed, ("yh", "head"), split_axis=0, concat_axis=0, tiled=True)
    banded = own[:, 256:]
    far2 = passed_along(jnp.concatenate([banded, own[128:, :256]], axis=0), "pair", 1)
    far4 = passed_along(banded, "pair", 2)
    win_dq, win_mine, win_back, sink_vals, bias, win_acc = window_call(
        sinks, segments.reshape(128, 128), win_q, win_dout, own, far2
    )
    win_dq, full_dq, band_mine, back2, back4, sink_rows = band_call(
        sink_vals, bias, full_q, full_dout, own, far2, far4, win_back, win_acc, win_dq
    )
    back2, back4 = passed_along(back2, "pair", -1), passed_along(back4, "pair", -2)
    sink_terms = lax.all_to_all(sink_rows, "pair", split_axis=0, concat_axis=0, tiled=True)
    summed = local_call(
        sum_kernel, shape((256, 640), BF16), (win_mine, band_mine, back2, back4, sink_terms), [VMEM] * 5
    )
    grads = lax.all_to_all(summed, ("yh", "head"), split_axis=0, concat_axis=0, tiled=True)
    win_dk, win_dv, full_dk, full_dv, sink_grads = local_call(
        unpack_kernel, (shape((32, 512), BF16),) * 4 + (shape((2, 16), F32),), (grads,), [VMEM]
    )
    return win_dq, win_dk, win_dv, full_dq, full_dk, full_dv, sink_grads


def solution(mesh):
    mesh = jax.sharding.Mesh(mesh.devices.reshape(PAIRS_OF_BLOCKS, 2, 4), ("pair", "yh", "head"))
    tokens = P(("pair", "yh"), "head")
    slices = P(("pair", "yh", "head"), None)
    in_specs = (tokens, slices, slices, tokens, tokens, slices, slices, tokens, P(None, "head"), P())
    out_specs = (tokens, slices, slices, tokens, slices, slices, P(None, "head"))
    return jax.shard_map(body, mesh=mesh, in_specs=in_specs, out_specs=out_specs, check_vma=False)
```

```python
import jax
import jax.numpy as jnp
from jax import lax
from jax.experimental import pallas as pl
from jax.experimental.pallas import tpu as pltpu
from jax.sharding import PartitionSpec as P

HEAD_DIM = 64
CYCLE = 4
BLOCK = 128
PAIRS = 4
NEG = -1e30
PAIRS_OF_BLOCKS = 64
VMEM = pl.BlockSpec(memory_space=pltpu.VMEM)
SMEM = pl.BlockSpec(memory_space=pltpu.SMEM)
ANY = pl.BlockSpec(memory_space=pl.ANY)
HBM = pl.BlockSpec(memory_space=pltpu.HBM)
BF16, F32 = jnp.bfloat16, jnp.float32


def passed_along(shard, axis, by):
    size = lax.axis_size(axis)
    pairs = [(i, i + by) for i in range(size) if 0 <= i + by < size]
    return lax.ppermute(shard, axis, pairs)


def low_lanes(rows):
    return lax.broadcasted_iota(jnp.int32, (rows, 128), 1) < 64


def both_ways(tile):
    turned = pltpu.roll(tile, 64, 1)
    low = low_lanes(tile.shape[0])
    return jnp.where(low, tile, turned), jnp.where(low, turned, tile)


def pair_rows(tile):
    low = low_lanes(128)
    zero = jnp.zeros_like(tile)
    return jnp.concatenate([jnp.where(low, tile, zero), jnp.where(low, zero, tile)], axis=0)


def dot(a, b, contract):
    return lax.dot_general(a, b, (contract, ((), ())), preferred_element_type=F32)


def build_bias(bias, seg_ref, me, blocks, windowed):
    seg_q = jnp.broadcast_to(seg_ref[pl.ds(me, 1), :], (128, 128))
    key_row = lax.broadcasted_iota(jnp.int32, (128, 128), 0)
    query_col = lax.broadcasted_iota(jnp.int32, (128, 128), 1)
    for b in range(blocks):
        lag = blocks - 1 - b
        at = me - lag
        seg_row = jnp.broadcast_to(seg_ref[pl.ds(jnp.maximum(at, 0), 1), :], (128, 128))
        seg_k = jnp.transpose(seg_row.astype(F32)).astype(jnp.int32)
        allowed = (seg_k == seg_q) & (at >= 0)
        if lag == 0:
            allowed = allowed & (key_row <= query_col)
        elif windowed:
            allowed = allowed & (key_row > query_col)
        tile = jnp.where(allowed, 0.0, NEG).astype(F32)
        bias[b * 128 : (b + 1) * 128, :] = jnp.concatenate([tile, tile], axis=1)


def layer(layer_id, sinks_ref, q_ref, do_ref, odd, places, bias, kd, vd, kt, ws, dss, dq_ref, sink_acc, send_sinks=None):
    blocks = len(places) - 1
    rows = blocks * 128

    def block(b, shift):
        first, second = (
            ref[row : row + 128, col + shift : col + shift + 128].astype(F32) for ref, row, col in places[b : b + 2]
        )
        return jnp.where(odd, second, first)

    for b in range(blocks):
        span = slice(b * 128, (b + 1) * 128)
        key = block(b, 0) * (HEAD_DIM**-0.5)
        k0, k1 = both_ways(key)
        kd[0, span, :] = k0.astype(BF16)
        kd[1, span, :] = k1.astype(BF16)
        turned = jnp.transpose(key).astype(BF16)
        kt[0, :, span] = turned[:64]
        kt[1, :, span] = turned[64:]
        v0, v1 = both_ways(block(b, 128))
        vd[0, span, :] = v0.astype(BF16)
        vd[1, span, :] = v1.astype(BF16)
    lane = lax.broadcasted_iota(jnp.int32, (1, 256), 1)
    sums = []
    for g in range(2):
        q2s, do2s = [], []
        for j in range(PAIRS):
            p = g * PAIRS + j
            q2 = pair_rows(q_ref[:, p * 128 : (p + 1) * 128])
            do2 = pair_rows(do_ref[:, p * 128 : (p + 1) * 128])
            q2s.append(q2)
            do2s.append(do2)
            sink = jnp.where(lane < 128, sinks_ref[layer_id : layer_id + 1, 2 * p : 2 * p + 1], sinks_ref[layer_id : layer_id + 1, 2 * p + 1 : 2 * p + 2])
            s = dot(kd[g, :rows, :], q2, ((1,), (1,))) + bias[:rows, :]
            m = jnp.maximum(jnp.max(s, axis=0, keepdims=True), sink)
            e = jnp.exp(s - m)
            sink_term = jnp.exp(sink - m)
            inverse = 1.0 / (jnp.sum(e, axis=0, keepdims=True) + sink_term)
            pr = e * inverse
            dp = dot(vd[g, :rows, :], do2, ((1,), (1,)))
            delta = jnp.sum(pr * dp, axis=0, keepdims=True)
            ws[:rows, j * 256 : (j + 1) * 256] = pr.astype(BF16)
            dss[:rows, j * 256 : (j + 1) * 256] = (pr * (dp - delta)).astype(BF16)
            grad = -(sink_term * inverse) * delta
            at = layer_id * 16 + 2 * p
            sink_acc[at : at + 1, :] = grad[:, :128]
            sink_acc[at + 1 : at + 2, :] = grad[:, 128:]
        if g == 1 and send_sinks is not None:
            send_sinks()
        q_all = jnp.concatenate(q2s, axis=0)
        do_all = jnp.concatenate(do2s, axis=0)
        dqt = dot(kt[g, :, :rows], dss[:rows, :], ((1,), (0,)))
        for j in range(PAIRS):
            p = g * PAIRS + j
            both = jnp.concatenate([dqt[:, j * 256 : j * 256 + 128], dqt[:, j * 256 + 128 : j * 256 + 256]], axis=0)
            dq_ref[:, p * 128 : (p + 1) * 128] = jnp.transpose(both).astype(BF16)
        dk = dot(dss[:rows, :], q_all, ((1,), (0,)))
        dv = dot(ws[:rows, :], do_all, ((1,), (0,)))
        sums.append((dk + pltpu.roll(dk, 64, 1), dv + pltpu.roll(dv, 64, 1)))
    low = low_lanes(rows)
    dk = jnp.where(low, sums[0][0], sums[1][0]) * (HEAD_DIM**-0.5)
    dv = jnp.where(low, sums[0][1], sums[1][1])
    return dk, dv


def shifted(grad, blocks, odd):
    zero = jnp.zeros((128, 128), F32)
    parts = [zero] + [grad[b * 128 : (b + 1) * 128] for b in range(blocks)] + [zero]
    return [jnp.where(odd, parts[b], parts[b + 1]) for b in range(blocks + 1)]


def window_kernel(
    sinks_hbm, seg_ref, q_ref, do_ref, own, far2,
    dq_ref, mine, back, sinks_ref, band_bias, sink_acc,
    bias, kd, vd, kt, ws, dss, sems,
):
    odd = lax.axis_index("yh") == 1
    me = lax.axis_index("pair") * 2 + lax.axis_index("yh")
    fetch = pltpu.make_async_copy(sinks_hbm, sinks_ref, sems.at[0])
    fetch.start()
    sink_acc[...] = jnp.zeros_like(sink_acc)
    build_bias(bias, seg_ref, me, 2, True)
    build_bias(band_bias, seg_ref, me, CYCLE + 1, False)
    fetch.wait()
    blocks = [(far2, 256, 0), (own, 0, 0), (own, 128, 0)]
    dk, dv = layer(
        0, sinks_ref, q_ref, do_ref, odd, blocks, bias, kd, vd, kt, ws, dss, dq_ref, sink_acc
    )
    for at, grad in ((0, dk), (128, dv)):
        parts = shifted(grad, 2, odd)
        back[:, at : at + 128] = parts[0].astype(BF16)
        mine[:128, at : at + 128] = parts[1]
        mine[128:, at : at + 128] = parts[2]


def band_kernel(
    sinks_ref, bias, q_ref, do_ref, own, far2, far4, win_back, win_acc, win_dq,
    win_dq_hbm, dq_ref, mine, back2, back4, sink_hbm,
    kd, vd, kt, ws, dss, sink_acc, sink_ref, sems,
):
    odd = lax.axis_index("yh") == 1
    win_send = pltpu.make_async_copy(win_dq, win_dq_hbm, sems.at[0])
    win_send.start()
    sink_acc[...] = win_acc[...]
    blocks = [(far4, 0, 0), (far4, 128, 0), (far2, 0, 0), (far2, 128, 0), (own, 0, 256), (own, 128, 256)]
    sink_send = pltpu.make_async_copy(sink_ref, sink_hbm, sems.at[1])

    def send_sinks():
        total = jnp.sum(jnp.transpose(sink_acc[...]), axis=0, keepdims=True)
        row = lax.broadcasted_iota(jnp.int32, sink_ref.shape, 0)
        sink_ref[...] = jnp.where(row % 2 == 0, total, 0.0)
        sink_send.start()

    dk, dv = layer(
        1, sinks_ref, q_ref, do_ref, odd, blocks, bias, kd, vd, kt, ws, dss, dq_ref, sink_acc, send_sinks
    )
    for at, grad in ((0, dk), (128, dv)):
        parts = shifted(grad, CYCLE + 1, odd)
        for half in range(2):
            rows = slice(half * 128, (half + 1) * 128)
            back4[rows, at : at + 128] = parts[half].astype(BF16)
            back2[rows, at : at + 128] = parts[2 + half].astype(BF16)
            mine[rows, at : at + 128] = parts[4 + half]
    back2[256:, :] = win_back[...]
    win_send.wait()
    sink_send.wait()


def scratch(rows):
    return [
        pltpu.VMEM((2, rows, 128), BF16),
        pltpu.VMEM((2, rows, 128), BF16),
        pltpu.VMEM((2, 64, rows), BF16),
        pltpu.VMEM((rows, 1024), BF16),
        pltpu.VMEM((rows, 1024), BF16),
        pltpu.VMEM((128, 1024), BF16),
    ]


def window_call(sinks, seg, q, do, own, far2):
    shape = jax.ShapeDtypeStruct
    return pl.pallas_call(
        window_kernel,
        out_shape=(
            shape((128, 1024), BF16), shape((256, 256), F32), shape((128, 256), BF16),
            shape((2, 16), F32), shape(((CYCLE + 1) * 128, 256), F32), shape((128, 128), F32),
        ),
        in_specs=[HBM] + [VMEM] * 5,
        out_specs=[VMEM] * 6,
        scratch_shapes=[pltpu.VMEM((256, 256), F32)] + scratch(256)[:-1] + [pltpu.SemaphoreType.DMA((1,))],
        compiler_params=pltpu.CompilerParams(vmem_limit_bytes=14 << 20),
        cost_estimate=pl.CostEstimate(flops=2_000_000_000, bytes_accessed=1_000_000, transcendentals=500_000),
    )(sinks, seg, q, do, own, far2)


def band_call(sinks, bias, q, do, own, far2, far4, win_back, win_acc, win_dq):
    shape = jax.ShapeDtypeStruct
    return pl.pallas_call(
        band_kernel,
        out_shape=(
            shape((128, 1024), BF16), shape((128, 1024), BF16),
            shape((256, 256), F32), shape((384, 256), BF16), shape((256, 256), BF16),
            shape((PAIRS_OF_BLOCKS * 2, 128), F32),
        ),
        in_specs=[VMEM] * 10,
        out_specs=[HBM] + [VMEM] * 4 + [HBM],
        scratch_shapes=scratch((CYCLE + 1) * 128)[:-1] + [pltpu.VMEM((128, 128), F32)] * 2 + [pltpu.SemaphoreType.DMA((2,))],
        compiler_params=pltpu.CompilerParams(vmem_limit_bytes=24 << 20),
        cost_estimate=pl.CostEstimate(flops=5_000_000_000, bytes_accessed=2_000_000, transcendentals=1_500_000),
    )(sinks, bias, q, do, own, far2, far4, win_back, win_acc, win_dq)


def pack_kernel(wk, wv, fk, fv, out, held, sems):
    copies = [pltpu.make_async_copy(ref, held.at[a], sems.at[a]) for a, ref in enumerate((wk, wv, fk, fv))]
    for copy in copies:
        copy.start()
    for a, copy in enumerate(copies):
        copy.wait()
        for t in range(8):
            h = t % 4
            out[t * 32 : (t + 1) * 32, a * 128 : (a + 1) * 128] = held[a, :, h * 128 : (h + 1) * 128]


def three_parts(row):
    high = row.astype(BF16).astype(F32)
    middle = (row - high).astype(BF16).astype(F32)
    low = row - high - middle
    at = lax.broadcasted_iota(jnp.int32, (16, 128), 0)
    rest = jnp.where(at == 2, low, 0.0)
    return jnp.where(at == 0, high, jnp.where(at == 1, middle, rest)).astype(BF16)


def sum_kernel(win_mine, band_mine, back2, back4, sink_terms, out):
    win = [win_mine[:128, :], win_mine[128:, :] + back2[256:, :].astype(F32)]
    sinks = three_parts(jnp.sum(sink_terms[...], axis=0, keepdims=True))
    for half in range(2):
        rows = slice(half * 128, (half + 1) * 128)
        band = (band_mine[rows, :] + back2[rows, :].astype(F32) + back4[rows, :].astype(F32)).astype(BF16)
        for t in range(4):
            at = (half * 4 + t) * 32
            out[at : at + 32, :256] = win[half][t * 32 : (t + 1) * 32].astype(BF16)
            out[at : at + 32, 256:512] = band[t * 32 : (t + 1) * 32]
            out[at : at + 16, 512:] = sinks
            out[at + 16 : at + 32, 512:] = jnp.zeros((16, 128), BF16)


def unpack_kernel(grads, dq_ref, wk, wv, fk, fv, sinks, dq_hbm, sem):
    send = pltpu.make_async_copy(dq_ref, dq_hbm, sem)
    send.start()

    def chunk(yh, t):
        at = (yh * 4 + t) * 32
        return grads[at : at + 32, :512].astype(F32)

    for t in range(4):
        total = (chunk(0, t) + chunk(1, t)).astype(BF16)
        for a, ref in enumerate((wk, wv, fk, fv)):
            ref[:, t * 128 : (t + 1) * 128] = total[:, a * 128 : (a + 1) * 128]
    parts = jnp.zeros((16, 128), F32)
    for yh in range(2):
        at = pl.multiple_of((yh * 4 + lax.axis_index("head")) * 32, 32)
        parts = parts + grads[pl.ds(at, 16), 512:].astype(F32)
    total = jnp.sum(parts, axis=0, keepdims=True)
    sinks[0:1, :] = total[:, 0:16]
    sinks[1:2, :] = total[:, 16:32]
    send.wait()


def local_call(kernel, out_shape, args, in_specs, scratch_shapes=(), flops=100_000, vmem=4):
    return pl.pallas_call(
        kernel,
        out_shape=out_shape,
        in_specs=in_specs,
        out_specs=jax.tree.map(lambda _: VMEM, out_shape),
        scratch_shapes=scratch_shapes,
        compiler_params=pltpu.CompilerParams(vmem_limit_bytes=vmem << 20),
        cost_estimate=pl.CostEstimate(flops=flops, bytes_accessed=500_000, transcendentals=0),
    )(*args)


def body(win_q, win_k, win_v, win_dout, full_q, full_k, full_v, full_dout, sinks, segments):
    shape = jax.ShapeDtypeStruct
    held = [pltpu.VMEM((4, 32, 512), BF16), pltpu.SemaphoreType.DMA((4,))]
    packed = local_call(pack_kernel, shape((256, 512), BF16), [pltpu.with_memory_space_constraint(x, pltpu.HBM) for x in (win_k, win_v, full_k, full_v)], [HBM] * 4, held)
    own = lax.all_to_all(packed, ("yh", "head"), split_axis=0, concat_axis=0, tiled=True)
    banded = own[:, 256:]
    far2 = passed_along(jnp.concatenate([banded, own[128:, :256]], axis=0), "pair", 1)
    far4 = passed_along(banded, "pair", 2)
    win_dq, win_mine, win_back, sink_vals, bias, win_acc = window_call(
        sinks, segments.reshape(128, 128), win_q, win_dout, own, far2
    )
    win_dq, band_dq, band_mine, back2, back4, sink_rows = band_call(
        sink_vals, bias, full_q, full_dout, own, far2, far4, win_back, win_acc, win_dq
    )
    back2, back4 = passed_along(back2, "pair", -1), passed_along(back4, "pair", -2)
    sink_terms = lax.all_to_all(sink_rows, "pair", split_axis=0, concat_axis=0, tiled=True)
    summed = local_call(
        sum_kernel, shape((256, 640), BF16), (win_mine, band_mine, back2, back4, sink_terms), [VMEM] * 5
    )
    grads = lax.all_to_all(summed, ("yh", "head"), split_axis=0, concat_axis=0, tiled=True)
    part = shape((32, 512), BF16)
    win_dk, win_dv, full_dk, full_dv, sink_grads, full_dq = pl.pallas_call(
        unpack_kernel,
        out_shape=(part,) * 4 + (shape((2, 16), F32), shape((128, 1024), BF16)),
        in_specs=[VMEM] * 2,
        out_specs=[VMEM] * 5 + [HBM],
        scratch_shapes=[pltpu.SemaphoreType.DMA],
        compiler_params=pltpu.CompilerParams(vmem_limit_bytes=4 << 20),
        cost_estimate=pl.CostEstimate(flops=100_000, bytes_accessed=500_000, transcendentals=0),
    )(grads, band_dq)
    return win_dq, win_dk, win_dv, full_dq, full_dk, full_dv, sink_grads


def solution(mesh):
    mesh = jax.sharding.Mesh(mesh.devices.reshape(PAIRS_OF_BLOCKS, 2, 4), ("pair", "yh", "head"))
    tokens = P(("pair", "yh"), "head")
    slices = P(("pair", "yh", "head"), None)
    in_specs = (tokens, slices, slices, tokens, tokens, slices, slices, tokens, P(None, "head"), P())
    out_specs = (tokens, slices, slices, tokens, slices, slices, P(None, "head"))
    return jax.shard_map(body, mesh=mesh, in_specs=in_specs, out_specs=out_specs, check_vma=False)
```
